256 devices in a mesh: row: 16 (over x, y), col: 16 (over z, core).
Axes of the slice: x: 4, y: 4, z: 8, core: 2. Of those that a mesh axis runs over, the one named last changes fastest.
Arguments:
- g_hist: bfloat16 [160, 160, 2, 128, 128], P('row', 'col'), may hold values from -6 to 6
- hamiltonian: float32 [2, 128, 128], replicated, may hold values from -0.5 to 0.5
- interaction: float32 [128], replicated, may hold values from 0.1 to 0.4
- partner: int32 [128], replicated, may hold values from 0 to 127, as said below
- order: int32 [160], replicated, may hold values from 0 to 159, each once
Outputs:
- new_row: float32 [160, 2, 128, 128], P('row', None, 'col')
The draws below stay inside these ranges and needn't reach their ends.
Inputs may be any that keep to these rules, and one draw needn't show every extreme that they name: partner[partner[a]] = a and partner[a] != a for every orbital a.
All inputs are finite; a program needn't handle non-finite values.
Results may differ from the reference program's by a relative error of at most 0.0025.
Values may be sent and summed in bfloat16 or wider, within the bound.
A program may use at most 64 MiB of HBM per device.

```python
import math
import jax
import jax.numpy as jnp
from jax import lax

O = 128
NT = 160


def draw_partner(key, part):
    key = jax.random.fold_in(key, 7)
    shuffled = jax.random.permutation(key, O).astype(jnp.int32)
    firsts = shuffled[0::2]
    seconds = shuffled[1::2]
    result = jnp.zeros((O,), jnp.int32).at[firsts].set(seconds)
    return result.at[seconds].set(firsts)


def level_of(rng, extent, pieces, smallest, largest):
    def one(position, shards_of):
        heights = jax.random.uniform(jax.random.fold_in(jax.random.fold_in(rng, 6), position), (shards_of,), jnp.float32, smallest / len(pieces), largest / len(pieces))
        return jnp.repeat(jnp.exp(heights), extent[position] // shards_of).reshape((-1,) + (1,) * (len(extent) - position - 1))

    level = one(*pieces[0])
    for cut in pieces[1:]:
        level = level * one(*cut)
    return level


def gaussian(key, shape, spread, reach, shards=(), kind=jnp.bfloat16):
    values = spread * jax.random.normal(key, shape, jnp.float32)
    if shards:
        values = values * level_of(key, shape, shards, -0.22, 0.18)
    return jnp.clip(values, -reach, reach).astype(kind)


def setup_inputs(seed: int = 0) -> dict:
    key_of = jax.random.split(jax.random.key(seed), 6)
    return {
        "g_hist": gaussian(key_of[0], (NT, NT, 2, O, O), 1.0, 6.0, ((0, 16), (1, 16))),
        "hamiltonian": gaussian(key_of[1], (2, O, O), O ** -0.5, 0.5, (), jnp.float32),
        "interaction": jnp.clip(jnp.exp(jax.random.uniform(key_of[2], (O,), jnp.float32, math.log(0.1), math.log(0.4))), 0.1, 0.4),
        "partner": draw_partner(jax.random.fold_in(key_of[5], 71), 0),
        "order": jax.random.permutation(key_of[4], NT).astype(jnp.int32),
    }


time_step = 0.1


def sigma_of(rows, interaction, partner):
    real = rows[:, 0].astype(jnp.float32)
    imag = rows[:, 1].astype(jnp.float32)
    magnitude = real * real + imag * imag
    swapped = magnitude[:, partner][:, :, partner]
    factor = -(interaction[:, None] * interaction[None, :])[None] * swapped
    return jnp.stack([factor * real, factor * imag], 1).astype(jnp.bfloat16)


def stack_terms(sig):
    real = sig[:, 0]
    imag = sig[:, 1]
    first = jnp.stack([-real, -imag], 1)
    second = jnp.stack([-imag, real], 1)
    return jnp.transpose(jnp.stack([first, second], 0), (3, 0, 1, 2, 4))


def integral(sig, g_hist, valid):
    stacked = stack_terms(sig)

    def one(pair):
        block, keep = pair
        masked = jnp.where(keep[:, None, None, None], block, jnp.zeros((), block.dtype))
        out = lax.dot_general(stacked, masked, (((2, 3, 4), (0, 1, 3)), ((), ())), preferred_element_type=jnp.float32)
        return time_step * jnp.transpose(out, (1, 0, 2))

    return lax.map(one, (g_hist, valid))


def apply_matrix(hamiltonian, field):
    high = lax.Precision.HIGHEST
    real = jnp.einsum("ac,kcb->kab", hamiltonian[0], field[:, 0], precision=high) - jnp.einsum("ac,kcb->kab", hamiltonian[1], field[:, 1], precision=high)
    imag = jnp.einsum("ac,kcb->kab", hamiltonian[0], field[:, 1], precision=high) + jnp.einsum("ac,kcb->kab", hamiltonian[1], field[:, 0], precision=high)
    return jnp.stack([real, imag], 1)


def reference(g_hist, hamiltonian, interaction, partner, order):
    total = order.shape[0]
    positions = jnp.arange(total, dtype=jnp.int32)
    latest = jnp.sum(jnp.where(order == total - 1, positions, 0)).astype(jnp.int32)
    column = lax.dynamic_index_in_dim(g_hist, latest, 1, keepdims=False)
    previous = jnp.stack([-jnp.swapaxes(column[:, 0], 1, 2), jnp.swapaxes(column[:, 1], 1, 2)], 1)
    valid = order[None, :] >= order[:, None]
    sigma_prev = sigma_of(previous, interaction, partner)
    memory_prev = integral(sigma_prev, g_hist, valid)
    prev_f = previous.astype(jnp.float32)
    hp = apply_matrix(hamiltonian, prev_f)
    predicted = jnp.stack([prev_f[:, 0] + time_step * hp[:, 1] + memory_prev[:, 1], prev_f[:, 1] - time_step * hp[:, 0] - memory_prev[:, 0]], 1).astype(jnp.bfloat16)
    sigma_new = sigma_of(predicted, interaction, partner)
    memory_new = integral(sigma_new, g_hist, valid)
    hg = apply_matrix(hamiltonian, predicted.astype(jnp.float32))
    real = prev_f[:, 0] + 0.5 * (time_step * (hp[:, 1] + hg[:, 1]) + memory_prev[:, 1] + memory_new[:, 1])
    imag = prev_f[:, 1] - 0.5 * (time_step * (hp[:, 0] + hg[:, 0]) + memory_prev[:, 0] + memory_new[:, 0])
    return jnp.stack([real, imag], 1)
```

```python
import functools

import jax
import jax.numpy as jnp
from jax import lax
from jax.experimental import pallas as pl
from jax.experimental.pallas import tpu as pltpu
from jax.sharding import PartitionSpec as P

MESH = pl.DeviceIdType.MESH
time_step = 0.1
O = 128
B = 10
ROWS = B * O
PIECE = ROWS // 16
HALF = ROWS // 2
FAR = (4, 3, 5, 2, 6, 1, 7)


def kernel(
    g_hbm, ham, inter, partner, order, out,
    g, send_a, core_a, z_a, piece_a, got_a, f_prev,
    w, wh, part_b, core_b, comb_b, z_b, piece_b, got_b, f_new,
    send_d, core_d, z_d,
    load_sem, core_ss, core_rs, z_ss, z_rs, t_ss, t_rs, all_ss, all_rs, loc_sem,
):
    r = lax.axis_index("row")
    c = lax.axis_index("col")
    z = c // 2
    k = c % 2
    other = (r, 2 * z + 1 - k)
    bf16 = jnp.bfloat16
    f32 = jnp.float32

    for j in range(B):
        pltpu.make_async_copy(g_hbm.at[j], g.at[j], load_sem.at[j]).start()

    barrier = pltpu.get_barrier_semaphore()
    peers = [other] + [(r, 2 * ((z + d) % 8) + k) for d in range(1, 8)]
    peers += [((r + d) % 16, c) for d in range(1, 16)]
    for peer in peers:
        pl.semaphore_signal(barrier, inc=1, device_id=peer, device_id_type=MESH)

    @pl.when(r != c)
    def _():
        pl.semaphore_signal(barrier, inc=1, device_id=(c, r), device_id_type=MESH)

    def find(i, found):
        for s in range(10):
            found = jnp.where(order[i * 10 + s] == 16 * B - 1, i * 10 + s, found)
        return found

    latest = lax.fori_loop(0, 16, find, jnp.int32(0))
    owner = latest // B
    within = latest - owner * B
    mine = jnp.where(owner == c, jnp.float32(1), jnp.float32(0)).astype(bf16)

    for j in range(B):
        pltpu.make_async_copy(g_hbm.at[j], g.at[j], load_sem.at[j]).wait()

    def column(j, carry):
        block = g[j, within]
        at = pl.ds(pl.multiple_of(j * O, O), O)
        send_a[at, :O] = -block[0] * mine
        send_a[at, O:] = block[1] * mine
        return carry

    lax.fori_loop(0, B, column, 0)

    @pl.when(r != c)
    def _():
        pl.semaphore_wait(barrier, len(peers) + 1)

    @pl.when(r == c)
    def _():
        pl.semaphore_wait(barrier, len(peers))

    def rows(start, size):
        return pl.ds(pl.multiple_of(start, 16), size)

    def remote(src, dst, ss, rs, to):
        return pltpu.make_async_remote_copy(
            src_ref=src, dst_ref=dst, send_sem=ss, recv_sem=rs, device_id=to, device_id_type=MESH
        )

    def z_sends(src_of, dst, phase):
        copies = []
        for d in FAR:
            zz = (z + d) % 8
            copy = remote(src_of(zz), dst.at[d], z_ss.at[phase, d], z_rs.at[phase, d], (r, 2 * zz + k))
            copy.start()
            copies.append(copy)
        return copies

    q = (r % 2) * 8 + r // 2

    def gather(piece, got, f, phase):
        @pl.when(r != c)
        def _():
            copy = remote(piece, got, t_ss.at[phase], t_rs.at[phase], (c, r))
            copy.start()
            copy.wait()

        @pl.when(r == c)
        def _():
            copy = pltpu.make_async_copy(piece, got, loc_sem.at[phase])
            copy.start()
            copy.wait()

        copies = []
        for d in range(1, 16):
            copy = remote(
                got, f.at[rows(q * PIECE, PIECE)], all_ss.at[phase, d], all_rs.at[phase, d], ((r + d) % 16, c)
            )
            copy.start()
            copies.append(copy)
        f[rows(q * PIECE, PIECE)] = got[...]
        return copies

    def gathered(copies):
        for copy in copies:
            copy.wait_recv()
        for copy in copies:
            copy.wait_send()

    a_core = remote(
        send_a.at[rows((1 - k) * HALF, HALF)], core_a, core_ss.at[0], core_rs.at[0], other
    )
    a_core.start()

    lane = lax.broadcasted_iota(jnp.int32, (O, O), 1)
    sub = lax.broadcasted_iota(jnp.int32, (O, O), 0)
    select = jnp.where(partner[...] == sub, jnp.float32(1), jnp.float32(0)).astype(bf16)
    u_row = inter[...]
    u_col = jnp.sum(jnp.where(lane == sub, jnp.broadcast_to(u_row, (O, O)), 0.0), axis=1, keepdims=True)
    strength = -(u_col * u_row)

    a_core.wait_recv()
    own = rows(k * HALF, HALF)
    send_a[own] = send_a[own] + core_a[...]
    a_z = z_sends(lambda zz: send_a.at[rows(k * HALF + zz * PIECE, PIECE)], z_a, 0)

    h_re = ham[0].T
    h_im = ham[1].T
    h_all = jnp.concatenate(
        [jnp.concatenate([h_im, -h_re], axis=1), jnp.concatenate([h_re, h_im], axis=1)], axis=0
    )
    high = h_all.astype(bf16)
    rest = h_all - high.astype(f32)
    mid = rest.astype(bf16)
    wh[0] = high
    wh[1] = mid
    wh[2] = (rest - mid.astype(f32)).astype(bf16)

    def mask(j, carry):
        row_time = order[r * B + j]
        for kk in range(B):
            keep = jnp.where(order[c * B + kk] >= row_time, jnp.float32(1), jnp.float32(0)).astype(bf16)
            g[j, kk] = g[j, kk] * keep
        return carry

    lax.fori_loop(0, B, mask, 0)

    total = send_a[rows(k * HALF + z * PIECE, PIECE)]
    for copy, d in zip(a_z, FAR):
        copy.wait_recv()
        total = total + z_a[d]
    piece_a[...] = total
    a_all = gather(piece_a, got_a, f_prev, 0)
    gathered(a_all)

    def self_energy(f):
        def one(n, carry):
            at = pl.ds(pl.multiple_of(n * O, O), O)
            re = f[at, :O]
            im = f[at, O:]
            both = jnp.concatenate([re, im], axis=0)
            turned = jnp.dot(both, select, preferred_element_type=f32).astype(bf16)
            turned = jnp.concatenate([turned[:O], turned[O:]], axis=1)
            turned = jnp.dot(select, turned, preferred_element_type=f32)
            t_re = turned[:, :O]
            t_im = turned[:, O:]
            factor = strength * (t_re * t_re + t_im * t_im)
            s_re = (factor * re.astype(f32)).astype(bf16)
            s_im = (factor * im.astype(f32)).astype(bf16)
            w[n, :O, :O] = -s_im
            w[n, :O, O:] = s_re
            w[n, O:, :O] = s_re
            w[n, O:, O:] = s_im
            return carry

        lax.fori_loop(0, B, one, 0)

    def contract(j):
        acc = jnp.zeros((O, 2 * O), f32)
        for kk in range(B):
            left = jnp.concatenate([g[j, kk, 0], g[j, kk, 1]], axis=1)
            acc += jnp.dot(left, w[kk], preferred_element_type=f32)
        return acc

    def hamiltonian(f, at):
        left = f[at]
        acc = jnp.dot(left, wh[2], preferred_element_type=f32)
        acc += jnp.dot(left, wh[1], preferred_element_type=f32)
        acc += jnp.dot(left, wh[0], preferred_element_type=f32)
        return acc

    self_energy(f_prev)

    def share_b(n, carry):
        j = ((1 - k) * 5 + n) % B
        at = pl.ds(pl.multiple_of(j * O, O), O)
        part_b[at] = time_step * contract(j)

        @pl.when(r == c)
        def _():
            part_b[at] += time_step * hamiltonian(f_prev, at) + f_prev[at].astype(f32)

        return carry

    lax.fori_loop(0, 5, share_b, 0)
    b_core = remote(
        part_b.at[rows((1 - k) * HALF, HALF)], core_b, core_ss.at[1], core_rs.at[1], other
    )
    b_core.start()
    lax.fori_loop(5, 10, share_b, 0)
    b_core.wait_recv()
    comb_b[...] = part_b[own] + core_b[...]
    b_z = z_sends(lambda zz: comb_b.at[rows(zz * PIECE, PIECE)], z_b, 1)
    total = comb_b[rows(z * PIECE, PIECE)]
    for copy, d in zip(b_z, FAR):
        copy.wait_recv()
        total = total + z_b[d]
    piece_b[...] = total.astype(bf16)
    b_all = gather(piece_b, got_b, f_new, 1)
    gathered(b_all)

    self_energy(f_new)

    def share_d(j, carry):
        at = pl.ds(pl.multiple_of(j * O, O), O)
        part_b[at] = 0.5 * part_b[at] + (0.5 * time_step) * contract(j)

        @pl.when(r == c)
        def _():
            part_b[at] += (0.5 * time_step) * hamiltonian(f_new, at) + 0.5 * f_prev[at].astype(f32)

        for o in range(2):
            turned = part_b[at, o * O:(o + 1) * O].T.reshape(8, 2, 8, O)
            for kk in range(2):
                send_d[kk, :, 2 * j + o] = turned[:, kk]
        return carry

    b_core.wait_send()
    lax.fori_loop(0, B, share_d, 0)
    d_core = remote(send_d.at[1 - k], core_d, core_ss.at[2], core_rs.at[2], other)
    d_core.start()
    d_core.wait()
    send_d[k] = send_d[k] + core_d[...]
    d_z = z_sends(lambda zz: send_d.at[k, zz], z_d, 2)
    total = send_d[k, z]
    for copy, d in zip(d_z, FAR):
        copy.wait_recv()
        total = total + z_d[d]
    out[...] = total.reshape(B, 2, 8, O)

    a_core.wait_send()
    for copies in (a_z, b_z, d_z):
        for copy in copies:
            copy.wait_send()


def shards(g_hist, hamiltonian, interaction, partner, order):
    bf16 = jnp.bfloat16
    f32 = jnp.float32
    vmem = pltpu.VMEM
    dma = pltpu.SemaphoreType.DMA
    spec = pl.BlockSpec(memory_space=pltpu.VMEM)
    return pl.pallas_call(
        kernel,
        out_shape=jax.ShapeDtypeStruct((B, 2, 8, O), f32),
        in_specs=[
            pl.BlockSpec(memory_space=pl.ANY),
            spec,
            spec,
            spec,
            pl.BlockSpec(memory_space=pltpu.SMEM),
        ],
        out_specs=spec,
        scratch_shapes=[
            vmem((B, B, 2, O, O), bf16),
            vmem((ROWS, 2 * O), bf16),
            vmem((HALF, 2 * O), bf16),
            vmem((8, PIECE, 2 * O), bf16),
            vmem((PIECE, 2 * O), bf16),
            vmem((PIECE, 2 * O), bf16),
            vmem((ROWS, 2 * O), bf16),
            vmem((B, 2 * O, 2 * O), bf16),
            vmem((3, 2 * O, 2 * O), bf16),
            vmem((ROWS, 2 * O), f32),
            vmem((HALF, 2 * O), f32),
            vmem((HALF, 2 * O), f32),
            vmem((8, PIECE, 2 * O), f32),
            vmem((PIECE, 2 * O), bf16),
            vmem((PIECE, 2 * O), bf16),
            vmem((ROWS, 2 * O), bf16),
            vmem((2, 8, 2 * B, 8, O), f32),
            vmem((8, 2 * B, 8, O), f32),
            vmem((8, 2 * B, 8, O), f32),
            dma((B,)),
            dma((3,)),
            dma((3,)),
            dma((3, 8)),
            dma((3, 8)),
            dma((2,)),
            dma((2,)),
            dma((2, 16)),
            dma((2, 16)),
            dma((2,)),
        ],
        compiler_params=pltpu.CompilerParams(
            collective_id=0, has_side_effects=True, vmem_limit_bytes=48 * 2**20
        ),
    )(g_hist, hamiltonian, interaction.reshape(1, O), partner.reshape(1, O), order)


def solution(mesh):
    in_specs = (P("row", "col", None, None, None), P(), P(), P(), P())
    out_specs = P("row", None, "col", None)
    return jax.shard_map(shards, mesh=mesh, in_specs=in_specs, out_specs=out_specs, check_vma=False)
```

```python
import jax
import jax.numpy as jnp
from jax import lax
from jax.experimental import pallas as pl
from jax.experimental.pallas import tpu as pltpu
from jax.sharding import PartitionSpec as P

MESH = pl.DeviceIdType.MESH
time_step = 0.1
O = 128
B = 10
ROWS = B * O
CHUNKS = ((0, 6), (6, 4))
NC = len(CHUNKS)
FAR = (4, 3, 5, 2, 6, 1, 7)
AROUND = sorted(
    ((dx, dy) for dx in range(4) for dy in range(4) if dx or dy),
    key=lambda o: -(min(o[0], 4 - o[0]) + min(o[1], 4 - o[1])),
)
STEP = (
    (2, 2), (1, 2), (2, 1), (2, 3), (2, 0), (1, 1), (3, 3), (0, 1),
    (3, 0), (0, 0), (0, 3), (1, 0), (1, 3), (3, 1), (3, 2), (0, 2),
)
STEP_X = tuple(s[0] for s in STEP)
STEP_Y = tuple(s[1] for s in STEP)
STEP_OF = tuple(STEP.index((i // 4, i % 4)) for i in range(16))


def look_up(table, index):
    value = jnp.int32(table[0])
    for i in range(1, len(table)):
        value = jnp.where(index == i, jnp.int32(table[i]), value)
    return value


def kernel(
    g_hbm, ham_hbm, inter_hbm, partner_hbm, order_hbm, out,
    g, ham, inter, partner, order,
    send_a, core_a, comb_a, z_a, piece_a, f_prev, w, wh, part,
    core_b, comb_b, z_b, sum_b, piece_b, f_new, z_d, sum_d,
    load_sem, small_sem, core_ss, core_rs, a_ss, a_rs, z_ss, z_rs, t_ss, t_rs, all_ss, all_rs, *chunked,
):
    bf16 = jnp.bfloat16
    f32 = jnp.float32
    r = lax.axis_index("row")
    c = lax.axis_index("col")
    x = r // 4
    y = r % 4
    z = c // 2
    k = c % 2
    other = (r, 2 * z + 1 - k)

    loads = [pltpu.make_async_copy(order_hbm, order, small_sem.at[0])]
    loads += [pltpu.make_async_copy(g_hbm.at[j], g.at[j], load_sem.at[j]) for j in range(B)]
    loads += [
        pltpu.make_async_copy(a, b, small_sem.at[i + 1])
        for i, (a, b) in enumerate(((ham_hbm, ham), (inter_hbm, inter), (partner_hbm, partner)))
    ]
    for load in loads:
        load.start()

    n_out = 2 * ((r // 2 - z + 8) % 8) + k
    to = ((x + look_up(STEP_X, n_out)) % 4 * 4 + (y + look_up(STEP_Y, n_out)) % 4, r)
    q_out = k * 8 + z
    n_in = look_up(STEP_OF, (x - c // 4 + 4) % 4 * 4 + (y - c % 4 + 4) % 4)
    z_in = (c // 2 - n_in // 2 + 8) % 8
    source = (c, 2 * z_in + n_in % 2)
    q_in = n_in % 2 * 8 + z_in
    around = [((x + dx) % 4 * 4 + (y + dy) % 4, c) for dx, dy in AROUND]

    barrier = pltpu.get_barrier_semaphore()
    up = (r, 2 * ((z + 1) % 8) + k)
    down = (r, 2 * ((z + 7) % 8) + k)
    peers = [to, source] + [(r, 2 * ((z + d) % 8) + k) for d in FAR] + around + [other]
    for peer in peers:
        pl.semaphore_signal(barrier, inc=1, device_id=peer, device_id_type=MESH)

    def rows(start, size):
        return pl.ds(pl.multiple_of(start, 16), size)

    def remote(src, dst, ss, rs, device):
        copy = pltpu.make_async_remote_copy(
            src_ref=src, dst_ref=dst, send_sem=ss, recv_sem=rs, device_id=device, device_id_type=MESH
        )
        copy.start()
        sent.append(copy)
        return copy

    sent = []
    send_d = chunked[:NC]
    core_d = chunked[NC:2 * NC]
    comb_d = chunked[2 * NC:]

    def half(ch, core):
        first, n = CHUNKS[ch]
        return rows(first * O + core * (n * O // 2), n * O // 2)

    def piece(ch, q):
        first, n = CHUNKS[ch]
        return rows(first * O + q * (n * 8), n * 8)

    def near(ch):
        first, n = CHUNKS[ch]
        return pl.ds(first * 8, n * 8)

    def core_near(ch):
        first, n = CHUNKS[ch]
        return pl.ds(first * 64, n * 64)

    def core_piece(ch, zz):
        first, n = CHUNKS[ch]
        return rows(first * 64 + zz * (n * 8), n * 8)

    def to_other(src, dst, phase, ch):
        return remote(src, dst, core_ss.at[phase, ch], core_rs.at[phase, ch], other)

    def chain(comb, own, slots, sums, box, halve, phase, ch, step):
        for way, (sign, device) in enumerate(((1, up), (7, down))):
            whole = own((z + sign * (4 - step)) % 8)
            if step == 0:
                src = comb.at[halve(whole, way)]
                dst = slots.at[(way, 0) + halve(box, way)]
            else:
                links[phase, ch, way, step - 1].wait_recv()
                sums[(way, step - 1) + box] = comb[whole]
                came = halve(box, way) if step == 1 else box
                there = (way, step - 1) + came
                sums[there] = sums[there] + slots[there]
                src = sums.at[(way, step - 1) + box]
                dst = slots.at[(way, step) + box]
            links[phase, ch, way, step] = remote(
                src, dst, z_ss.at[phase, ch, way, step], z_rs.at[phase, ch, way, step], device
            )

    def chained(comb, own, slots, box, phase, ch):
        total = comb[own(z)]
        for way in range(2):
            links[phase, ch, way, 3].wait_recv()
            total = total + slots[(way, 3) + box]
        return total

    links = {}

    def lane_half(index, way):
        return index + (pl.ds(way * O, O),)

    def turn(src, f, phase, ch):
        return remote(src, f.at[piece(ch, q_out)], t_ss.at[phase, ch], t_rs.at[phase, ch], to)

    def spread(f, phase, ch):
        return [
            remote(
                f.at[piece(ch, q_in)], f.at[piece(ch, q_in)],
                all_ss.at[phase, ch, i], all_rs.at[phase, ch, i], device,
            )
            for i, device in enumerate(around)
        ]

    def received(copies):
        for copy in copies:
            copy.wait_recv()

    loads[0].wait()

    def find(i, found):
        for s in range(B):
            found = jnp.where(order[i * B + s] == 16 * B - 1, i * B + s, found)
        return found

    latest = lax.fori_loop(0, 16, find, jnp.int32(0))
    owner = latest // B
    within = latest - owner * B
    mine = jnp.where(owner == c, jnp.float32(1), jnp.float32(0)).astype(bf16)

    for load in loads[1:]:
        load.wait()

    for j in range(B):
        block = g[j, within]
        send_a[j * O:(j + 1) * O, :O] = -block[0] * mine
        send_a[j * O:(j + 1) * O, O:] = block[1] * mine

    pl.semaphore_wait(barrier, len(peers))

    a_core = [
        to_other(send_a.at[half(ch, 1 - k)], core_a.at[core_near(ch)], 0, ch) for ch in range(NC)
    ]

    a_z = []
    for ch in range(NC):
        a_core[ch].wait_recv()
        comb_a[core_near(ch)] = send_a[half(ch, k)] + core_a[core_near(ch)]
        a_z.append([
            remote(
                comb_a.at[core_piece(ch, (z + d) % 8)], z_a.at[d - 1, near(ch)],
                a_ss.at[ch, d - 1], a_rs.at[ch, d - 1], (r, 2 * ((z + d) % 8) + k),
            )
            for d in FAR
        ])

    lane = lax.broadcasted_iota(jnp.int32, (O, O), 1)
    sub = lax.broadcasted_iota(jnp.int32, (O, O), 0)
    select = jnp.where(partner[...] == sub, jnp.float32(1), jnp.float32(0)).astype(bf16)
    u_row = inter[...]
    u_col = jnp.sum(
        jnp.where(lane == sub, jnp.broadcast_to(u_row, (O, O)), 0.0), axis=1, keepdims=True
    )
    strength = -(u_col * u_row)
    h_re = ham[0].T
    h_im = ham[1].T
    h_all = jnp.concatenate(
        [jnp.concatenate([h_im, -h_re], axis=1), jnp.concatenate([h_re, h_im], axis=1)], axis=0
    )
    high = h_all.astype(bf16)
    rest = h_all - high.astype(f32)
    mid = rest.astype(bf16)
    wh[0] = high
    wh[1] = mid
    wh[2] = (rest - mid.astype(f32)).astype(bf16)

    def mask(j, carry):
        row_time = order[r * B + j]
        for kk in range(B):
            keep = jnp.where(order[c * B + kk] >= row_time, jnp.float32(1), jnp.float32(0)).astype(bf16)
            g[j, kk] = g[j, kk] * keep
        return carry

    lax.fori_loop(0, B, mask, 0)

    def hamiltonian(left):
        acc = jnp.dot(left, wh[2], preferred_element_type=f32)
        acc += jnp.dot(left, wh[1], preferred_element_type=f32)
        acc += jnp.dot(left, wh[0], preferred_element_type=f32)
        return acc

    def flow(finish, f, phase):
        turns = []
        spreads = []
        for ch in range(NC):
            finish(ch)
            turns.append(turn((piece_a, piece_b)[phase].at[near(ch)], f, phase, ch))
            if ch > 0:
                turns[ch - 1].wait_recv()
                spreads.append(spread(f, phase, ch - 1))
        turns[NC - 1].wait_recv()
        spreads.append(spread(f, phase, NC - 1))
        return spreads

    def finish_a(ch):
        total = comb_a[core_piece(ch, z)]
        for copy, d in zip(a_z[ch], FAR):
            copy.wait_recv()
            total = total + z_a[d - 1, near(ch)]
        piece_a[near(ch)] = total

    a_all = flow(finish_a, f_prev, 0)

    def self_energy(f, ch):
        first, count = CHUNKS[ch]
        for n in range(first, first + count):
            re = f[n * O:(n + 1) * O, :O]
            im = f[n * O:(n + 1) * O, O:]
            both = jnp.concatenate([re, im], axis=0)
            turned = jnp.dot(both, select, preferred_element_type=f32).astype(bf16)
            turned = jnp.concatenate([turned[:O], turned[O:]], axis=1)
            turned = jnp.dot(select, turned, preferred_element_type=f32)
            t_re = turned[:, :O]
            t_im = turned[:, O:]
            factor = strength * (t_re * t_re + t_im * t_im)
            s_re = (factor * re.astype(f32)).astype(bf16)
            s_im = (factor * im.astype(f32)).astype(bf16)
            w[n, :O, :O] = -s_im
            w[n, :O, O:] = s_re
            w[n, O:, :O] = s_re
            w[n, O:, O:] = s_im

    def contract(first, count, ch, fresh):
        at = rows(first * O, count * O)
        start, number = CHUNKS[ch]
        for kk in range(start, start + number):
            left = jnp.concatenate(
                [g[pl.ds(first, count), kk, i].reshape(count * O, O) for i in range(2)], axis=1
            )
            term = jnp.dot(left, w[kk], preferred_element_type=f32)
            if fresh and kk == start:
                part[at] = term
            else:
                part[at] += term

    for ch in range(NC):
        received(a_all[ch])
        self_energy(f_prev, ch)
        if ch < NC - 1:
            contract(0, B, ch, ch == 0)
    b_core = []

    def chain_b(ch, step):
        chain(
            comb_b, lambda zz: (core_piece(ch, zz),), z_b, sum_b, (near(ch),), lane_half, 1, ch, step
        )

    for ch in range(NC):
        first, n = CHUNKS[ch]
        contract(first + (1 - k) * (n // 2), n // 2, NC - 1, False)
        b_core.append(to_other(part.at[half(ch, 1 - k)], core_b.at[core_near(ch)], 1, ch))
        contract(first + k * (n // 2), n // 2, NC - 1, False)
        b_core[ch].wait_recv()
        comb_b[core_near(ch)] = part[half(ch, k)] + core_b[core_near(ch)]
        chain_b(ch, 0)
    for step in range(1, 4):
        for ch in range(NC):
            chain_b(ch, step)
    for copy in b_core:
        copy.wait_send()
    sent[:] = [copy for copy in sent if not any(copy is done for done in b_core)]

    def finish_b(ch):
        first, n = CHUNKS[ch]
        base = piece_a[near(ch)]
        shift = hamiltonian(base)
        total = chained(comb_b, lambda zz: (core_piece(ch, zz),), z_b, (near(ch),), 1, ch)
        base = base.astype(f32)
        new = (base + time_step * (shift + total)).astype(bf16)
        piece_b[near(ch)] = new
        part[piece(ch, q_out)] += (2 / time_step) * base + shift + hamiltonian(new)

    b_all = flow(finish_b, f_new, 1)

    for ch in range(NC):
        received(b_all[ch])
        self_energy(f_new, ch)
        if ch < NC - 1:
            contract(0, B, ch, False)
    d_core = []

    def box_d(ch):
        first, n = CHUNKS[ch]
        return (pl.ds(first * 16, n * 16),)

    def chain_d(ch, step):
        first, n = CHUNKS[ch]

        def row_half(index, way):
            start = first * 16 if len(index) == 1 else 0
            return index[:-1] + (pl.ds(start + way * n * 8, n * 8),)

        chain(
            comb_d[ch], lambda zz: (zz, pl.ds(0, n * 16)), z_d, sum_d, box_d(ch), row_half, 2, ch, step
        )

    def over_z_d(ch):
        first, n = CHUNKS[ch]
        d_core[ch].wait_recv()
        comb_d[ch][...] = send_d[ch][k] + core_d[ch][...]
        chain_d(ch, 0)

    for ch in range(NC):
        first, n = CHUNKS[ch]
        contract(first, n, NC - 1, False)
        for j in range(first, first + n):
            for o in range(2):
                turned = part[j * O:(j + 1) * O, o * O:(o + 1) * O].T.reshape(8, 2, 8, O)
                at = pl.ds((2 * (j - first) + o) * 8, 8)
                for kk in range(2):
                    send_d[ch][kk, :, at] = turned[:, kk]
        d_core.append(to_other(send_d[ch].at[1 - k], core_d[ch], 2, ch))
        if ch > 0:
            over_z_d(ch - 1)
    over_z_d(NC - 1)
    for step in range(1, 4):
        for ch in range(NC):
            chain_d(ch, step)
    for ch in range(NC):
        first, n = CHUNKS[ch]
        total = chained(comb_d[ch], lambda zz: (zz, pl.ds(0, n * 16)), z_d, box_d(ch), 2, ch)
        out[first:first + n] = (0.5 * time_step) * total.reshape(n, 2, 8, O)

    for copy in sent:
        copy.wait_send()


def shards(g_hist, hamiltonian, interaction, partner, order):
    bf16 = jnp.bfloat16
    f32 = jnp.float32
    vmem = pltpu.VMEM
    dma = pltpu.SemaphoreType.DMA
    return pl.pallas_call(
        kernel,
        out_shape=jax.ShapeDtypeStruct((B, 2, 8, O), f32),
        in_specs=[pl.BlockSpec(memory_space=pltpu.HBM)] * 5,
        out_specs=pl.BlockSpec(memory_space=pltpu.VMEM),
        scratch_shapes=[
            vmem((B, B, 2, O, O), bf16),
            vmem((2, O, O), f32),
            vmem((1, O), f32),
            vmem((1, O), jnp.int32),
            pltpu.SMEM((16 * B,), jnp.int32),
            vmem((ROWS, 2 * O), bf16),
            vmem((ROWS // 2, 2 * O), bf16),
            vmem((ROWS // 2, 2 * O), bf16),
            vmem((7, ROWS // 16, 2 * O), bf16),
            vmem((ROWS // 16, 2 * O), bf16),
            vmem((ROWS, 2 * O), bf16),
            vmem((B, 2 * O, 2 * O), bf16),
            vmem((3, 2 * O, 2 * O), bf16),
            vmem((ROWS, 2 * O), f32),
            vmem((ROWS // 2, 2 * O), f32),
            vmem((ROWS // 2, 2 * O), f32),
            vmem((2, 4, ROWS // 16, 2 * O), f32),
            vmem((2, 3, ROWS // 16, 2 * O), f32),
            vmem((ROWS // 16, 2 * O), bf16),
            vmem((ROWS, 2 * O), bf16),
            vmem((2, 4, 16 * B, O), f32),
            vmem((2, 3, 16 * B, O), f32),
            dma((B,)),
            dma((4,)),
            dma((3, NC)),
            dma((3, NC)),
            dma((NC, 7)),
            dma((NC, 7)),
            dma((3, NC, 2, 4)),
            dma((3, NC, 2, 4)),
            dma((2, NC)),
            dma((2, NC)),
            dma((2, NC, 15)),
            dma((2, NC, 15)),
        ]
        + [vmem((2, 8, 16 * n, O), f32) for _, n in CHUNKS]
        + [vmem((8, 16 * n, O), f32) for _, n in CHUNKS] * 2,
        compiler_params=pltpu.CompilerParams(
            collective_id=0, has_side_effects=True, vmem_limit_bytes=60 * 2**20
        ),
    )(g_hist, hamiltonian, interaction.reshape(1, O), partner.reshape(1, O), order)


def solution(mesh):
    in_specs = (P("row", "col", None, None, None), P(), P(), P(), P())
    out_specs = P("row", None, "col", None)
    return jax.shard_map(shards, mesh=mesh, in_specs=in_specs, out_specs=out_specs, check_vma=False)
```

```python
import jax
import jax.numpy as jnp
from jax import lax
from jax.experimental import pallas as pl
from jax.experimental.pallas import tpu as pltpu
from jax.sharding import PartitionSpec as P

MESH = pl.DeviceIdType.MESH
time_step = 0.1
O = 128
LEVELS = 32766.0
B = 10
ROWS = B * O
CHUNKS = ((0, 6), (6, 4))
NC = len(CHUNKS)
FAR = (4, 3, 5, 2, 6, 1, 7)
AROUND = sorted(
    ((dx, dy) for dx in range(4) for dy in range(4) if dx or dy),
    key=lambda o: -(min(o[0], 4 - o[0]) + min(o[1], 4 - o[1])),
)
STEP = (
    (2, 2), (1, 2), (2, 1), (2, 3), (2, 0), (1, 1), (3, 3), (0, 1),
    (3, 0), (0, 0), (0, 3), (1, 0), (1, 3), (3, 1), (3, 2), (0, 2),
)
STEP_X = tuple(s[0] for s in STEP)
STEP_Y = tuple(s[1] for s in STEP)
STEP_OF = tuple(STEP.index((i // 4, i % 4)) for i in range(16))


def look_up(table, index):
    value = jnp.int32(table[0])
    for i in range(1, len(table)):
        value = jnp.where(index == i, jnp.int32(table[i]), value)
    return value


def kernel(
    g_hbm, ham_hbm, inter_hbm, partner_hbm, order_hbm, out,
    g, ham, inter, partner, order,
    send_a, core_a, comb_a, z_a, piece_a, f_prev, w, wh, part,
    core_b, comb_b, code_b, z_b, scale, scales, shift_b, piece_b, f_new, code_d, z_d,
    load_sem, small_sem, core_ss, core_rs, a_ss, a_rs, s_ss, s_rs, z_ss, z_rs, t_ss, t_rs, all_ss, all_rs, *chunked,
):
    bf16 = jnp.bfloat16
    f32 = jnp.float32
    r = lax.axis_index("row")
    c = lax.axis_index("col")
    x = r // 4
    y = r % 4
    z = c // 2
    k = c % 2
    other = (r, 2 * z + 1 - k)

    loads = [pltpu.make_async_copy(order_hbm, order, small_sem.at[0])]
    loads += [pltpu.make_async_copy(g_hbm.at[j], g.at[j], load_sem.at[j]) for j in range(B)]
    loads += [
        pltpu.make_async_copy(a, b, small_sem.at[i + 1])
        for i, (a, b) in enumerate(((ham_hbm, ham), (inter_hbm, inter), (partner_hbm, partner)))
    ]
    for load in loads:
        load.start()

    n_out = 2 * ((r // 2 - z + 8) % 8) + k
    to = ((x + look_up(STEP_X, n_out)) % 4 * 4 + (y + look_up(STEP_Y, n_out)) % 4, r)
    q_out = k * 8 + z
    n_in = look_up(STEP_OF, (x - c // 4 + 4) % 4 * 4 + (y - c % 4 + 4) % 4)
    z_in = (c // 2 - n_in // 2 + 8) % 8
    source = (c, 2 * z_in + n_in % 2)
    q_in = n_in % 2 * 8 + z_in
    around = [((x + dx) % 4 * 4 + (y + dy) % 4, c) for dx, dy in AROUND]

    barrier = pltpu.get_barrier_semaphore()
    peers = [to, source] + [(r, 2 * ((z + d) % 8) + k) for d in FAR] + around + [other]
    for peer in peers:
        pl.semaphore_signal(barrier, inc=1, device_id=peer, device_id_type=MESH)

    def rows(start, size):
        return pl.ds(pl.multiple_of(start, 16), size)

    def remote(src, dst, ss, rs, device):
        copy = pltpu.make_async_remote_copy(
            src_ref=src, dst_ref=dst, send_sem=ss, recv_sem=rs, device_id=device, device_id_type=MESH
        )
        copy.start()
        sent.append(copy)
        return copy

    sent = []
    send_d = chunked[:NC]
    core_d = chunked[NC:2 * NC]
    comb_d = chunked[2 * NC:]

    def half(ch, core):
        first, n = CHUNKS[ch]
        return rows(first * O + core * (n * O // 2), n * O // 2)

    def piece(ch, q):
        first, n = CHUNKS[ch]
        return rows(first * O + q * (n * 8), n * 8)

    def near(ch):
        first, n = CHUNKS[ch]
        return pl.ds(first * 8, n * 8)

    def core_near(ch):
        first, n = CHUNKS[ch]
        return pl.ds(first * 64, n * 64)

    def core_piece(ch, zz):
        first, n = CHUNKS[ch]
        return rows(first * 64 + zz * (n * 8), n * 8)

    def to_other(src, dst, phase, ch):
        return remote(src, dst, core_ss.at[phase, ch], core_rs.at[phase, ch], other)

    def code(piece_of, rows_at, coded, scale, phase, ch):
        for zz in range(8):
            term = piece_of(zz)
            most = jnp.max(jnp.max(jnp.abs(term), axis=0, keepdims=True), axis=1, keepdims=True)
            most = jnp.maximum(most, 1e-30)
            term = term * (LEVELS / most)
            coded[zz, rows_at] = (term + jnp.where(term >= 0, 0.5, -0.5)).astype(jnp.int32).astype(jnp.int16)
            scale[phase, ch, zz] = jnp.broadcast_to(most * (1 / LEVELS), (8, O))

    def over_z(coded, rows_at, slots, phase, ch):
        copies = []
        for d in FAR:
            zz = (z + d) % 8
            device = (r, 2 * zz + k)
            copies.append((
                d,
                remote(
                    scale.at[phase, ch, zz], scales.at[phase, ch, d - 1],
                    s_ss.at[phase, ch, d - 1], s_rs.at[phase, ch, d - 1], device,
                ),
                remote(
                    coded.at[zz, rows_at], slots.at[d - 1, rows_at],
                    z_ss.at[phase, ch, d - 1], z_rs.at[phase, ch, d - 1], device,
                ),
            ))
        return copies

    def summed(total, copies, rows_at, slots, phase, ch):
        for d, first_copy, second_copy in copies:
            first_copy.wait_recv()
            second_copy.wait_recv()
            unit = scales[phase, ch, d - 1, :1]
            if total.shape[1] > O:
                unit = jnp.concatenate([unit, unit], axis=1)
            total = total + slots[d - 1, rows_at].astype(jnp.int32).astype(f32) * unit
        return total

    def turn(src, f, phase, ch):
        return remote(src, f.at[piece(ch, q_out)], t_ss.at[phase, ch], t_rs.at[phase, ch], to)

    def spread(f, phase, ch):
        return [
            remote(
                f.at[piece(ch, q_in)], f.at[piece(ch, q_in)],
                all_ss.at[phase, ch, i], all_rs.at[phase, ch, i], device,
            )
            for i, device in enumerate(around)
        ]

    def received(copies):
        for copy in copies:
            copy.wait_recv()

    loads[0].wait()

    def find(i, found):
        for s in range(B):
            found = jnp.where(order[i * B + s] == 16 * B - 1, i * B + s, found)
        return found

    latest = lax.fori_loop(0, 16, find, jnp.int32(0))
    owner = latest // B
    within = latest - owner * B
    mine = jnp.where(owner == c, jnp.float32(1), jnp.float32(0)).astype(bf16)

    for load in loads[1:]:
        load.wait()

    for j in range(B):
        block = g[j, within]
        send_a[j * O:(j + 1) * O, :O] = -block[0] * mine
        send_a[j * O:(j + 1) * O, O:] = block[1] * mine

    pl.semaphore_wait(barrier, len(peers))

    a_core = [
        to_other(send_a.at[half(ch, 1 - k)], core_a.at[core_near(ch)], 0, ch) for ch in range(NC)
    ]

    a_z = []
    for ch in range(NC):
        a_core[ch].wait_recv()
        comb_a[core_near(ch)] = send_a[half(ch, k)] + core_a[core_near(ch)]
        a_z.append([
            remote(
                comb_a.at[core_piece(ch, (z + d) % 8)], z_a.at[d - 1, near(ch)],
                a_ss.at[ch, d - 1], a_rs.at[ch, d - 1], (r, 2 * ((z + d) % 8) + k),
            )
            for d in FAR
        ])

    lane = lax.broadcasted_iota(jnp.int32, (O, O), 1)
    sub = lax.broadcasted_iota(jnp.int32, (O, O), 0)
    select = jnp.where(partner[...] == sub, jnp.float32(1), jnp.float32(0)).astype(bf16)
    u_row = inter[...]
    u_col = jnp.sum(
        jnp.where(lane == sub, jnp.broadcast_to(u_row, (O, O)), 0.0), axis=1, keepdims=True
    )
    strength = -(u_col * u_row)
    h_re = ham[0].T
    h_im = ham[1].T
    h_all = jnp.concatenate(
        [jnp.concatenate([h_im, -h_re], axis=1), jnp.concatenate([h_re, h_im], axis=1)], axis=0
    )
    high = h_all.astype(bf16)
    rest = h_all - high.astype(f32)
    mid = rest.astype(bf16)
    wh[0] = high
    wh[1] = mid
    wh[2] = (rest - mid.astype(f32)).astype(bf16)

    def mask(j, carry):
        row_time = order[r * B + j]
        for kk in range(B):
            keep = jnp.where(order[c * B + kk] >= row_time, jnp.float32(1), jnp.float32(0)).astype(bf16)
            g[j, kk] = g[j, kk] * keep
        return carry

    lax.fori_loop(0, B, mask, 0)

    def hamiltonian(left):
        acc = jnp.dot(left, wh[2], preferred_element_type=f32)
        acc += jnp.dot(left, wh[1], preferred_element_type=f32)
        acc += jnp.dot(left, wh[0], preferred_element_type=f32)
        return acc

    def flow(finish, f, phase, after):
        turns = []
        spreads = []
        for ch in range(NC):
            finish(ch)
            turns.append(turn((piece_a, piece_b)[phase].at[near(ch)], f, phase, ch))
            if ch > 0:
                turns[ch - 1].wait_recv()
                spreads.append(spread(f, phase, ch - 1))
        turns[NC - 1].wait_recv()
        spreads.append(spread(f, phase, NC - 1))
        for ch in range(NC):
            after(ch)
        return spreads

    def finish_a(ch):
        total = comb_a[core_piece(ch, z)]
        for copy, d in zip(a_z[ch], FAR):
            copy.wait_recv()
            total = total + z_a[d - 1, near(ch)]
        piece_a[near(ch)] = total

    def after_a(ch):
        base = piece_a[near(ch)]
        shift_b[near(ch)] = hamiltonian(base)

    a_all = flow(finish_a, f_prev, 0, after_a)

    def self_energy(f, ch):
        first, count = CHUNKS[ch]
        for n in range(first, first + count):
            re = f[n * O:(n + 1) * O, :O]
            im = f[n * O:(n + 1) * O, O:]
            both = jnp.concatenate([re, im], axis=0)
            turned = jnp.dot(both, select, preferred_element_type=f32).astype(bf16)
            turned = jnp.concatenate([turned[:O], turned[O:]], axis=1)
            turned = jnp.dot(select, turned, preferred_element_type=f32)
            t_re = turned[:, :O]
            t_im = turned[:, O:]
            factor = strength * (t_re * t_re + t_im * t_im)
            s_re = (factor * re.astype(f32)).astype(bf16)
            s_im = (factor * im.astype(f32)).astype(bf16)
            w[n, :O, :O] = -s_im
            w[n, :O, O:] = s_re
            w[n, O:, :O] = s_re
            w[n, O:, O:] = s_im

    def contract(first, count, ch, fresh):
        at = rows(first * O, count * O)
        start, number = CHUNKS[ch]
        for kk in range(start, start + number):
            left = jnp.concatenate(
                [g[pl.ds(first, count), kk, i].reshape(count * O, O) for i in range(2)], axis=1
            )
            term = jnp.dot(left, w[kk], preferred_element_type=f32)
            if fresh and kk == start:
                part[at] = term
            else:
                part[at] += term

    for ch in range(NC):
        received(a_all[ch])
        self_energy(f_prev, ch)
        if ch < NC - 1:
            contract(0, B, ch, ch == 0)
    b_core = []

    b_z = []
    for ch in range(NC):
        first, n = CHUNKS[ch]
        contract(first + (1 - k) * (n // 2), n // 2, NC - 1, False)
        b_core.append(to_other(part.at[half(ch, 1 - k)], core_b.at[core_near(ch)], 1, ch))
        contract(first + k * (n // 2), n // 2, NC - 1, False)
        b_core[ch].wait_recv()
        comb_b[core_near(ch)] = part[half(ch, k)] + core_b[core_near(ch)]
        code(
            lambda zz: comb_b[first * 64 + zz * n * 8:first * 64 + (zz + 1) * n * 8],
            near(ch), code_b, scale, 0, ch,
        )
        b_z.append(over_z(code_b, near(ch), z_b, 0, ch))
    for copy in b_core:
        copy.wait_send()
    sent[:] = [copy for copy in sent if not any(copy is done for done in b_core)]

    def finish_b(ch):
        first, n = CHUNKS[ch]
        total = summed(comb_b[core_piece(ch, z)], b_z[ch], near(ch), z_b, 0, ch)
        base = piece_a[near(ch)].astype(f32)
        piece_b[near(ch)] = (base + time_step * (shift_b[near(ch)] + total)).astype(bf16)

    def after_b(ch):
        base = piece_a[near(ch)].astype(f32)
        rest = (2 / time_step) * base + shift_b[near(ch)] + hamiltonian(piece_b[near(ch)])
        part[piece(ch, q_out)] += rest

    b_all = flow(finish_b, f_new, 1, after_b)

    for ch in range(NC):
        received(b_all[ch])
        self_energy(f_new, ch)
        if ch < NC - 1:
            contract(0, B, ch, False)
    d_core = []

    d_z = []

    def over_z_d(ch):
        first, n = CHUNKS[ch]
        d_core[ch].wait_recv()
        comb_d[ch][...] = send_d[ch][k] + core_d[ch][...]
        at = pl.ds(first * 16, n * 16)
        code(lambda zz: comb_d[ch][zz], at, code_d, scale, 1, ch)
        d_z.append(over_z(code_d, at, z_d, 1, ch))

    for ch in range(NC):
        first, n = CHUNKS[ch]
        contract(first, n, NC - 1, False)
        for j in range(first, first + n):
            for o in range(2):
                turned = part[j * O:(j + 1) * O, o * O:(o + 1) * O].T.reshape(8, 2, 8, O)
                at = pl.ds((2 * (j - first) + o) * 8, 8)
                for kk in range(2):
                    send_d[ch][kk, :, at] = turned[:, kk]
        d_core.append(to_other(send_d[ch].at[1 - k], core_d[ch], 2, ch))
        if ch > 0:
            over_z_d(ch - 1)
    over_z_d(NC - 1)
    for ch in range(NC):
        first, n = CHUNKS[ch]
        total = summed(comb_d[ch][z], d_z[ch], pl.ds(first * 16, n * 16), z_d, 1, ch)
        out[first:first + n] = (0.5 * time_step) * total.reshape(n, 2, 8, O)

    for copy in sent:
        copy.wait_send()


def shards(g_hist, hamiltonian, interaction, partner, order):
    bf16 = jnp.bfloat16
    f32 = jnp.float32
    vmem = pltpu.VMEM
    dma = pltpu.SemaphoreType.DMA
    return pl.pallas_call(
        kernel,
        out_shape=jax.ShapeDtypeStruct((B, 2, 8, O), f32),
        in_specs=[pl.BlockSpec(memory_space=pltpu.HBM)] * 5,
        out_specs=pl.BlockSpec(memory_space=pltpu.VMEM),
        scratch_shapes=[
            vmem((B, B, 2, O, O), bf16),
            vmem((2, O, O), f32),
            vmem((1, O), f32),
            vmem((1, O), jnp.int32),
            pltpu.SMEM((16 * B,), jnp.int32),
            vmem((ROWS, 2 * O), bf16),
            vmem((ROWS // 2, 2 * O), bf16),
            vmem((ROWS // 2, 2 * O), bf16),
            vmem((7, ROWS // 16, 2 * O), bf16),
            vmem((ROWS // 16, 2 * O), bf16),
            vmem((ROWS, 2 * O), bf16),
            vmem((B, 2 * O, 2 * O), bf16),
            vmem((3, 2 * O, 2 * O), bf16),
            vmem((ROWS, 2 * O), f32),
            vmem((ROWS // 2, 2 * O), f32),
            vmem((ROWS // 2, 2 * O), f32),
            vmem((8, ROWS // 16, 2 * O), jnp.int16),
            vmem((7, ROWS // 16, 2 * O), jnp.int16),
            vmem((2, NC, 8, 8, O), f32),
            vmem((2, NC, 7, 8, O), f32),
            vmem((ROWS // 16, 2 * O), f32),
            vmem((ROWS // 16, 2 * O), bf16),
            vmem((ROWS, 2 * O), bf16),
            vmem((8, 16 * B, O), jnp.int16),
            vmem((7, 16 * B, O), jnp.int16),
            dma((B,)),
            dma((4,)),
            dma((3, NC)),
            dma((3, NC)),
            dma((NC, 7)),
            dma((NC, 7)),
            dma((2, NC, 7)),
            dma((2, NC, 7)),
            dma((2, NC, 7)),
            dma((2, NC, 7)),
            dma((2, NC)),
            dma((2, NC)),
            dma((2, NC, 15)),
            dma((2, NC, 15)),
        ]
        + [vmem((2, 8, 16 * n, O), f32) for _, n in CHUNKS]
        + [vmem((8, 16 * n, O), f32) for _, n in CHUNKS] * 2,
        compiler_params=pltpu.CompilerParams(
            collective_id=0, has_side_effects=True, vmem_limit_bytes=60 * 2**20
        ),
    )(g_hist, hamiltonian, interaction.reshape(1, O), partner.reshape(1, O), order)


def solution(mesh):
    in_specs = (P("row", "col", None, None, None), P(), P(), P(), P())
    out_specs = P("row", None, "col", None)
    return jax.shard_map(shards, mesh=mesh, in_specs=in_specs, out_specs=out_specs, check_vma=False)
```

```python
import jax
import jax.numpy as jnp
from jax import lax
from jax.experimental import pallas as pl
from jax.experimental.pallas import tpu as pltpu
from jax.sharding import PartitionSpec as P

MESH = pl.DeviceIdType.MESH
time_step = 0.1
O = 128
LEVELS = 32766.0
B = 10
ROWS = B * O
CHUNKS = ((0, 4), (4, 6))
NC = len(CHUNKS)
FAR = (4, 3, 5, 2, 6, 1, 7)
AROUND = sorted(
    ((dx, dy) for dx in range(4) for dy in range(4) if dx or dy),
    key=lambda o: -(min(o[0], 4 - o[0]) + min(o[1], 4 - o[1])),
)
STEP = (
    (2, 2), (1, 2), (2, 1), (2, 3), (2, 0), (1, 1), (3, 3), (0, 1),
    (3, 0), (0, 0), (0, 3), (1, 0), (1, 3), (3, 1), (3, 2), (0, 2),
)
STEP_X = tuple(s[0] for s in STEP)
STEP_Y = tuple(s[1] for s in STEP)
STEP_OF = tuple(STEP.index((i // 4, i % 4)) for i in range(16))


def look_up(table, index):
    value = jnp.int32(table[0])
    for i in range(1, len(table)):
        value = jnp.where(index == i, jnp.int32(table[i]), value)
    return value


def kernel(
    g_hbm, ham_hbm, inter_hbm, partner_hbm, order_hbm, out,
    g, ham, inter, partner, order,
    send_a, core_a, comb_a, z_a, piece_a, f_prev, w, wh, part,
    core_b, comb_b, code_b, z_b, scale, scales, shift_b, piece_b, f_new, code_d, z_d,
    load_sem, small_sem, core_ss, core_rs, a_ss, a_rs, s_ss, s_rs, z_ss, z_rs, t_ss, t_rs, all_ss, all_rs, *chunked,
):
    bf16 = jnp.bfloat16
    f32 = jnp.float32
    r = lax.axis_index("row")
    c = lax.axis_index("col")
    x = r // 4
    y = r % 4
    z = c // 2
    k = c % 2
    other = (r, 2 * z + 1 - k)

    loads = [pltpu.make_async_copy(order_hbm, order, small_sem.at[0])]
    loads += [pltpu.make_async_copy(g_hbm.at[j], g.at[j], load_sem.at[j]) for j in range(B)]
    loads += [
        pltpu.make_async_copy(a, b, small_sem.at[i + 1])
        for i, (a, b) in enumerate(((ham_hbm, ham), (inter_hbm, inter), (partner_hbm, partner)))
    ]
    for load in loads:
        load.start()

    n_out = 2 * ((r // 2 - z + 8) % 8) + k
    to = ((x + look_up(STEP_X, n_out)) % 4 * 4 + (y + look_up(STEP_Y, n_out)) % 4, r)
    q_out = k * 8 + z
    n_in = look_up(STEP_OF, (x - c // 4 + 4) % 4 * 4 + (y - c % 4 + 4) % 4)
    z_in = (c // 2 - n_in // 2 + 8) % 8
    source = (c, 2 * z_in + n_in % 2)
    q_in = n_in % 2 * 8 + z_in
    around = [((x + dx) % 4 * 4 + (y + dy) % 4, c) for dx, dy in AROUND]

    barrier = pltpu.get_barrier_semaphore()
    peers = [to, source] + [(r, 2 * ((z + d) % 8) + k) for d in FAR] + around + [other]
    for peer in peers:
        pl.semaphore_signal(barrier, inc=1, device_id=peer, device_id_type=MESH)

    def rows(start, size):
        return pl.ds(pl.multiple_of(start, 16), size)

    def remote(src, dst, ss, rs, device):
        copy = pltpu.make_async_remote_copy(
            src_ref=src, dst_ref=dst, send_sem=ss, recv_sem=rs, device_id=device, device_id_type=MESH
        )
        copy.start()
        sent.append(copy)
        return copy

    sent = []
    send_d = chunked[:NC]
    core_d = chunked[NC:2 * NC]
    comb_d = chunked[2 * NC:]

    def half(ch, core):
        first, n = CHUNKS[ch]
        return rows(first * O + core * (n * O // 2), n * O // 2)

    def piece(ch, q):
        first, n = CHUNKS[ch]
        return rows(first * O + q * (n * 8), n * 8)

    def near(ch):
        first, n = CHUNKS[ch]
        return pl.ds(first * 8, n * 8)

    def core_near(ch):
        first, n = CHUNKS[ch]
        return pl.ds(first * 64, n * 64)

    def core_piece(ch, zz):
        first, n = CHUNKS[ch]
        return rows(first * 64 + zz * (n * 8), n * 8)

    def to_other(src, dst, phase, ch):
        return remote(src, dst, core_ss.at[phase, ch], core_rs.at[phase, ch], other)

    def code(piece_of, rows_at, coded, scale, phase, ch):
        for zz in range(8):
            term = piece_of(zz)
            most = jnp.max(jnp.max(jnp.abs(term), axis=0, keepdims=True), axis=1, keepdims=True)
            most = jnp.maximum(most, 1e-30)
            term = term * (LEVELS / most)
            coded[zz, rows_at] = (term + jnp.where(term >= 0, 0.5, -0.5)).astype(jnp.int32).astype(jnp.int16)
            scale[phase, ch, zz] = jnp.broadcast_to(most * (1 / LEVELS), (8, O))

    def over_z(coded, rows_at, slots, phase, ch):
        copies = []
        for d in FAR:
            zz = (z + d) % 8
            device = (r, 2 * zz + k)
            copies.append((
                d,
                remote(
                    scale.at[phase, ch, zz], scales.at[phase, ch, d - 1],
                    s_ss.at[phase, ch, d - 1], s_rs.at[phase, ch, d - 1], device,
                ),
                remote(
                    coded.at[zz, rows_at], slots.at[d - 1, rows_at],
                    z_ss.at[phase, ch, d - 1], z_rs.at[phase, ch, d - 1], device,
                ),
            ))
        return copies

    def summed(total, copies, rows_at, slots, phase, ch):
        for d, first_copy, second_copy in copies:
            first_copy.wait_recv()
            second_copy.wait_recv()
            unit = scales[phase, ch, d - 1, :1]
            if total.shape[1] > O:
                unit = jnp.concatenate([unit, unit], axis=1)
            total = total + slots[d - 1, rows_at].astype(jnp.int32).astype(f32) * unit
        return total

    def turn(src, f, phase, ch):
        return remote(src, f.at[piece(ch, q_out)], t_ss.at[phase, ch], t_rs.at[phase, ch], to)

    def spread(f, phase, ch):
        return [
            remote(
                f.at[piece(ch, q_in)], f.at[piece(ch, q_in)],
                all_ss.at[phase, ch, i], all_rs.at[phase, ch, i], device,
            )
            for i, device in enumerate(around)
        ]

    def received(copies):
        for copy in copies:
            copy.wait_recv()

    loads[0].wait()

    def find(i, found):
        for s in range(B):
            found = jnp.where(order[i * B + s] == 16 * B - 1, i * B + s, found)
        return found

    latest = lax.fori_loop(0, 16, find, jnp.int32(0))
    owner = latest // B
    within = latest - owner * B
    mine = jnp.where(owner == c, jnp.float32(1), jnp.float32(0)).astype(bf16)

    for load in loads[1:]:
        load.wait()

    for j in range(B):
        block = g[j, within]
        send_a[j * O:(j + 1) * O, :O] = -block[0] * mine
        send_a[j * O:(j + 1) * O, O:] = block[1] * mine

    pl.semaphore_wait(barrier, len(peers))

    a_core = [
        to_other(send_a.at[half(ch, 1 - k)], core_a.at[core_near(ch)], 0, ch) for ch in range(NC)
    ]

    a_z = []
    for ch in range(NC):
        a_core[ch].wait_recv()
        comb_a[core_near(ch)] = send_a[half(ch, k)] + core_a[core_near(ch)]
        a_z.append([
            remote(
                comb_a.at[core_piece(ch, (z + d) % 8)], z_a.at[d - 1, near(ch)],
                a_ss.at[ch, d - 1], a_rs.at[ch, d - 1], (r, 2 * ((z + d) % 8) + k),
            )
            for d in FAR
        ])

    lane = lax.broadcasted_iota(jnp.int32, (O, O), 1)
    sub = lax.broadcasted_iota(jnp.int32, (O, O), 0)
    select = jnp.where(partner[...] == sub, jnp.float32(1), jnp.float32(0)).astype(bf16)
    u_row = inter[...]
    u_col = jnp.sum(
        jnp.where(lane == sub, jnp.broadcast_to(u_row, (O, O)), 0.0), axis=1, keepdims=True
    )
    strength = -(u_col * u_row)
    h_re = ham[0].T
    h_im = ham[1].T
    h_all = jnp.concatenate(
        [jnp.concatenate([h_im, -h_re], axis=1), jnp.concatenate([h_re, h_im], axis=1)], axis=0
    )
    high = h_all.astype(bf16)
    rest = h_all - high.astype(f32)
    mid = rest.astype(bf16)
    wh[0] = high
    wh[1] = mid
    wh[2] = (rest - mid.astype(f32)).astype(bf16)

    def mask(j, carry):
        row_time = order[r * B + j]
        for kk in range(B):
            keep = jnp.where(order[c * B + kk] >= row_time, jnp.float32(1), jnp.float32(0)).astype(bf16)
            g[j, kk] = g[j, kk] * keep
        return carry

    lax.fori_loop(0, B, mask, 0)

    def hamiltonian(left):
        acc = jnp.dot(left, wh[2], preferred_element_type=f32)
        acc += jnp.dot(left, wh[1], preferred_element_type=f32)
        acc += jnp.dot(left, wh[0], preferred_element_type=f32)
        return acc

    def flow(finish, f, phase, after):
        turns = []
        spreads = []
        for ch in range(NC):
            finish(ch)
            turns.append(turn((piece_a, piece_b)[phase].at[near(ch)], f, phase, ch))
            if ch > 0:
                turns[ch - 1].wait_recv()
                spreads.append(spread(f, phase, ch - 1))
        turns[NC - 1].wait_recv()
        spreads.append(spread(f, phase, NC - 1))
        for ch in range(NC):
            after(ch)
        return spreads

    def finish_a(ch):
        total = comb_a[core_piece(ch, z)]
        for copy, d in zip(a_z[ch], FAR):
            copy.wait_recv()
            total = total + z_a[d - 1, near(ch)]
        piece_a[near(ch)] = total

    def after_a(ch):
        base = piece_a[near(ch)]
        shift_b[near(ch)] = hamiltonian(base)

    a_all = flow(finish_a, f_prev, 0, after_a)

    def self_energy(f, ch):
        first, count = CHUNKS[ch]
        for n in range(first, first + count):
            re = f[n * O:(n + 1) * O, :O]
            im = f[n * O:(n + 1) * O, O:]
            both = jnp.concatenate([re, im], axis=0)
            turned = jnp.dot(both, select, preferred_element_type=f32).astype(bf16)
            turned = jnp.concatenate([turned[:O], turned[O:]], axis=1)
            turned = jnp.dot(select, turned, preferred_element_type=f32)
            t_re = turned[:, :O]
            t_im = turned[:, O:]
            factor = strength * (t_re * t_re + t_im * t_im)
            s_re = (factor * re.astype(f32)).astype(bf16)
            s_im = (factor * im.astype(f32)).astype(bf16)
            w[n, :O, :O] = -s_im
            w[n, :O, O:] = s_re
            w[n, O:, :O] = s_re
            w[n, O:, O:] = s_im

    def contract(first, count, ch, fresh):
        at = rows(first * O, count * O)
        start, number = CHUNKS[ch]
        for kk in range(start, start + number):
            left = jnp.concatenate(
                [g[pl.ds(first, count), kk, i].reshape(count * O, O) for i in range(2)], axis=1
            )
            term = jnp.dot(left, w[kk], preferred_element_type=f32)
            if fresh and kk == start:
                part[at] = term
            else:
                part[at] += term

    for ch in range(NC):
        received(a_all[ch])
        self_energy(f_prev, ch)
        if ch < NC - 1:
            contract(0, B, ch, ch == 0)
    b_core = []

    b_z = []
    for ch in range(NC):
        first, n = CHUNKS[ch]
        contract(first + (1 - k) * (n // 2), n // 2, NC - 1, False)
        b_core.append(to_other(part.at[half(ch, 1 - k)], core_b.at[core_near(ch)], 1, ch))
    for ch in range(NC):
        first, n = CHUNKS[ch]
        contract(first + k * (n // 2), n // 2, NC - 1, False)
        b_core[ch].wait_recv()
        comb_b[core_near(ch)] = part[half(ch, k)] + core_b[core_near(ch)]
        code(
            lambda zz: comb_b[first * 64 + zz * n * 8:first * 64 + (zz + 1) * n * 8],
            near(ch), code_b, scale, 0, ch,
        )
        b_z.append(over_z(code_b, near(ch), z_b, 0, ch))
    for copy in b_core:
        copy.wait_send()
    sent[:] = [copy for copy in sent if not any(copy is done for done in b_core)]

    def finish_b(ch):
        first, n = CHUNKS[ch]
        total = summed(comb_b[core_piece(ch, z)], b_z[ch], near(ch), z_b, 0, ch)
        base = piece_a[near(ch)].astype(f32)
        piece_b[near(ch)] = (base + time_step * (shift_b[near(ch)] + total)).astype(bf16)

    def after_b(ch):
        base = piece_a[near(ch)].astype(f32)
        rest = (2 / time_step) * base + shift_b[near(ch)] + hamiltonian(piece_b[near(ch)])
        part[piece(ch, q_out)] += rest

    b_all = flow(finish_b, f_new, 1, after_b)

    for ch in range(NC):
        received(b_all[ch])
        self_energy(f_new, ch)
        if ch < NC - 1:
            contract(0, B, ch, False)
    d_core = []

    d_z = []

    def over_z_d(ch):
        first, n = CHUNKS[ch]
        d_core[ch].wait_recv()
        comb_d[ch][...] = send_d[ch][k] + core_d[ch][...]
        at = pl.ds(first * 16, n * 16)
        code(lambda zz: comb_d[ch][zz], at, code_d, scale, 1, ch)
        d_z.append(over_z(code_d, at, z_d, 1, ch))

    for ch in range(NC):
        first, n = CHUNKS[ch]
        if ch > 0:
            over_z_d(ch - 1)
        contract(first, n, NC - 1, False)
        for j in range(first, first + n):
            for o in range(2):
                turned = part[j * O:(j + 1) * O, o * O:(o + 1) * O].T.reshape(8, 2, 8, O)
                at = pl.ds((2 * (j - first) + o) * 8, 8)
                for kk in range(2):
                    send_d[ch][kk, :, at] = turned[:, kk]
        d_core.append(to_other(send_d[ch].at[1 - k], core_d[ch], 2, ch))
    over_z_d(NC - 1)
    for ch in range(NC):
        first, n = CHUNKS[ch]
        total = summed(comb_d[ch][z], d_z[ch], pl.ds(first * 16, n * 16), z_d, 1, ch)
        out[first:first + n] = (0.5 * time_step) * total.reshape(n, 2, 8, O)

    for copy in sent:
        copy.wait_send()


def shards(g_hist, hamiltonian, interaction, partner, order):
    bf16 = jnp.bfloat16
    f32 = jnp.float32
    vmem = pltpu.VMEM
    dma = pltpu.SemaphoreType.DMA
    return pl.pallas_call(
        kernel,
        out_shape=jax.ShapeDtypeStruct((B, 2, 8, O), f32),
        in_specs=[pl.BlockSpec(memory_space=pltpu.HBM)] * 5,
        out_specs=pl.BlockSpec(memory_space=pltpu.VMEM),
        scratch_shapes=[
            vmem((B, B, 2, O, O), bf16),
            vmem((2, O, O), f32),
            vmem((1, O), f32),
            vmem((1, O), jnp.int32),
            pltpu.SMEM((16 * B,), jnp.int32),
            vmem((ROWS, 2 * O), bf16),
            vmem((ROWS // 2, 2 * O), bf16),
            vmem((ROWS // 2, 2 * O), bf16),
            vmem((7, ROWS // 16, 2 * O), bf16),
            vmem((ROWS // 16, 2 * O), bf16),
            vmem((ROWS, 2 * O), bf16),
            vmem((B, 2 * O, 2 * O), bf16),
            vmem((3, 2 * O, 2 * O), bf16),
            vmem((ROWS, 2 * O), f32),
            vmem((ROWS // 2, 2 * O), f32),
            vmem((ROWS // 2, 2 * O), f32),
            vmem((8, ROWS // 16, 2 * O), jnp.int16),
            vmem((7, ROWS // 16, 2 * O), jnp.int16),
            vmem((2, NC, 8, 8, O), f32),
            vmem((2, NC, 7, 8, O), f32),
            vmem((ROWS // 16, 2 * O), f32),
            vmem((ROWS // 16, 2 * O), bf16),
            vmem((ROWS, 2 * O), bf16),
            vmem((8, 16 * B, O), jnp.int16),
            vmem((7, 16 * B, O), jnp.int16),
            dma((B,)),
            dma((4,)),
            dma((3, NC)),
            dma((3, NC)),
            dma((NC, 7)),
            dma((NC, 7)),
            dma((2, NC, 7)),
            dma((2, NC, 7)),
            dma((2, NC, 7)),
            dma((2, NC, 7)),
            dma((2, NC)),
            dma((2, NC)),
            dma((2, NC, 15)),
            dma((2, NC, 15)),
        ]
        + [vmem((2, 8, 16 * n, O), f32) for _, n in CHUNKS]
        + [vmem((8, 16 * n, O), f32) for _, n in CHUNKS] * 2,
        compiler_params=pltpu.CompilerParams(
            collective_id=0, has_side_effects=True, vmem_limit_bytes=60 * 2**20
        ),
    )(g_hist, hamiltonian, interaction.reshape(1, O), partner.reshape(1, O), order)


def solution(mesh):
    in_specs = (P("row", "col", None, None, None), P(), P(), P(), P())
    out_specs = P("row", None, "col", None)
    return jax.shard_map(shards, mesh=mesh, in_specs=in_specs, out_specs=out_specs, check_vma=False)
```

```python
import jax
import jax.numpy as jnp
from jax import lax
from jax.experimental import pallas as pl
from jax.experimental.pallas import tpu as pltpu
from jax.sharding import PartitionSpec as P

MESH = pl.DeviceIdType.MESH
time_step = 0.1
O = 128
LEVELS = 32766.0
B = 10
ROWS = B * O
CHUNKS = ((0, 4), (4, 6))
NC = len(CHUNKS)
FAR = (4, 3, 5, 2, 6, 1, 7)
AROUND = sorted(
    ((dx, dy) for dx in range(4) for dy in range(4) if dx or dy),
    key=lambda o: -(min(o[0], 4 - o[0]) + min(o[1], 4 - o[1])),
)
STEP = (
    (2, 2), (1, 2), (2, 1), (2, 3), (2, 0), (1, 1), (3, 3), (0, 1),
    (3, 0), (0, 0), (0, 3), (1, 0), (1, 3), (3, 1), (3, 2), (0, 2),
)
STEP_X = tuple(s[0] for s in STEP)
STEP_Y = tuple(s[1] for s in STEP)
STEP_OF = tuple(STEP.index((i // 4, i % 4)) for i in range(16))


def look_up(table, index):
    value = jnp.int32(table[0])
    for i in range(1, len(table)):
        value = jnp.where(index == i, jnp.int32(table[i]), value)
    return value


def kernel(
    g_hbm, ham_hbm, inter_hbm, partner_hbm, order_hbm, out,
    g, ham, inter, partner, order,
    send_a, core_a, comb_a, z_a, piece_a, f_prev, w, wh, part,
    core_b, comb_b, code_b, z_b, scale, scales, shift_b, piece_b, f_new, code_d, z_d,
    load_sem, small_sem, core_ss, core_rs, a_ss, a_rs, s_ss, s_rs, z_ss, z_rs, t_ss, t_rs, all_ss, all_rs, *chunked,
):
    bf16 = jnp.bfloat16
    f32 = jnp.float32
    r = lax.axis_index("row")
    c = lax.axis_index("col")
    x = r // 4
    y = r % 4
    z = c // 2
    k = c % 2
    other = (r, 2 * z + 1 - k)

    loads = [pltpu.make_async_copy(order_hbm, order, small_sem.at[0])]
    loads += [pltpu.make_async_copy(g_hbm.at[j], g.at[j], load_sem.at[j]) for j in range(B)]
    loads += [
        pltpu.make_async_copy(a, b, small_sem.at[i + 1])
        for i, (a, b) in enumerate(((ham_hbm, ham), (inter_hbm, inter), (partner_hbm, partner)))
    ]
    n_out = 2 * ((r // 2 - z + 8) % 8) + k
    to = ((x + look_up(STEP_X, n_out)) % 4 * 4 + (y + look_up(STEP_Y, n_out)) % 4, r)
    q_out = k * 8 + z
    n_in = look_up(STEP_OF, (x - c // 4 + 4) % 4 * 4 + (y - c % 4 + 4) % 4)
    z_in = (c // 2 - n_in // 2 + 8) % 8
    source = (c, 2 * z_in + n_in % 2)
    q_in = n_in % 2 * 8 + z_in
    around = [((x + dx) % 4 * 4 + (y + dy) % 4, c) for dx, dy in AROUND]

    barrier = pltpu.get_barrier_semaphore()
    peers = [to, source] + [(r, 2 * ((z + d) % 8) + k) for d in FAR] + around + [other]
    for peer in peers:
        pl.semaphore_signal(barrier, inc=1, device_id=peer, device_id_type=MESH)
    for load in loads:
        load.start()

    def rows(start, size):
        return pl.ds(pl.multiple_of(start, 16), size)

    def remote(src, dst, ss, rs, device):
        copy = pltpu.make_async_remote_copy(
            src_ref=src, dst_ref=dst, send_sem=ss, recv_sem=rs, device_id=device, device_id_type=MESH
        )
        copy.start()
        sent.append(copy)
        return copy

    sent = []
    send_d = chunked[:NC]
    core_d = chunked[NC:2 * NC]
    comb_d = chunked[2 * NC:]

    def half(ch, core):
        first, n = CHUNKS[ch]
        return rows(first * O + core * (n * O // 2), n * O // 2)

    def piece(ch, q):
        first, n = CHUNKS[ch]
        return rows(first * O + q * (n * 8), n * 8)

    def near(ch):
        first, n = CHUNKS[ch]
        return pl.ds(first * 8, n * 8)

    def core_near(ch):
        first, n = CHUNKS[ch]
        return pl.ds(first * 64, n * 64)

    def core_piece(ch, zz):
        first, n = CHUNKS[ch]
        return rows(first * 64 + zz * (n * 8), n * 8)

    def to_other(src, dst, phase, ch):
        return remote(src, dst, core_ss.at[phase, ch], core_rs.at[phase, ch], other)

    def code(piece_of, rows_at, coded, scale, phase, ch):
        for zz in range(8):
            term = piece_of(zz)
            most = jnp.max(jnp.max(jnp.abs(term), axis=0, keepdims=True), axis=1, keepdims=True)
            most = jnp.maximum(most, 1e-30)
            term = term * (LEVELS / most)
            coded[zz, rows_at] = (term + jnp.where(term >= 0, 0.5, -0.5)).astype(jnp.int32).astype(jnp.int16)
            scale[phase, ch, zz] = jnp.broadcast_to(most * (1 / LEVELS), (8, O))

    def over_z(coded, rows_at, slots, phase, ch):
        copies = []
        for d in FAR:
            zz = (z + d) % 8
            device = (r, 2 * zz + k)
            copies.append((
                d,
                remote(
                    scale.at[phase, ch, zz], scales.at[phase, ch, d - 1],
                    s_ss.at[phase, ch, d - 1], s_rs.at[phase, ch, d - 1], device,
                ),
                remote(
                    coded.at[zz, rows_at], slots.at[d - 1, rows_at],
                    z_ss.at[phase, ch, d - 1], z_rs.at[phase, ch, d - 1], device,
                ),
            ))
        return copies

    def summed(total, copies, rows_at, slots, phase, ch):
        for d, first_copy, second_copy in copies:
            first_copy.wait_recv()
            second_copy.wait_recv()
            unit = scales[phase, ch, d - 1, :1]
            if total.shape[1] > O:
                unit = jnp.concatenate([unit, unit], axis=1)
            total = total + slots[d - 1, rows_at].astype(jnp.int32).astype(f32) * unit
        return total

    def turn(src, f, phase, ch):
        return remote(src, f.at[piece(ch, q_out)], t_ss.at[phase, ch], t_rs.at[phase, ch], to)

    def spread(f, phase, ch):
        return [
            remote(
                f.at[piece(ch, q_in)], f.at[piece(ch, q_in)],
                all_ss.at[phase, ch, i], all_rs.at[phase, ch, i], device,
            )
            for i, device in enumerate(around)
        ]

    def received(copies):
        for copy in copies:
            copy.wait_recv()

    loads[0].wait()

    def find(i, found):
        for s in range(B):
            found = jnp.where(order[i * B + s] == 16 * B - 1, i * B + s, found)
        return found

    latest = lax.fori_loop(0, 16, find, jnp.int32(0))
    owner = latest // B
    within = latest - owner * B
    mine = jnp.where(owner == c, jnp.float32(1), jnp.float32(0)).astype(bf16)

    for load in loads[1:]:
        load.wait()

    for j in range(B):
        block = g[j, within]
        send_a[j * O:(j + 1) * O, :O] = -block[0] * mine
        send_a[j * O:(j + 1) * O, O:] = block[1] * mine

    pl.semaphore_wait(barrier, len(peers))

    a_core = [
        to_other(send_a.at[half(ch, 1 - k)], core_a.at[core_near(ch)], 0, ch) for ch in range(NC)
    ]

    a_z = []
    for ch in range(NC):
        a_core[ch].wait_recv()
        comb_a[core_near(ch)] = send_a[half(ch, k)] + core_a[core_near(ch)]
        a_z.append([
            remote(
                comb_a.at[core_piece(ch, (z + d) % 8)], z_a.at[d - 1, near(ch)],
                a_ss.at[ch, d - 1], a_rs.at[ch, d - 1], (r, 2 * ((z + d) % 8) + k),
            )
            for d in FAR
        ])

    lane = lax.broadcasted_iota(jnp.int32, (O, O), 1)
    sub = lax.broadcasted_iota(jnp.int32, (O, O), 0)
    select = jnp.where(partner[...] == sub, jnp.float32(1), jnp.float32(0)).astype(bf16)
    u_row = inter[...]
    u_col = jnp.sum(
        jnp.where(lane == sub, jnp.broadcast_to(u_row, (O, O)), 0.0), axis=1, keepdims=True
    )
    strength = -(u_col * u_row)
    h_re = ham[0].T
    h_im = ham[1].T
    h_all = jnp.concatenate(
        [jnp.concatenate([h_im, -h_re], axis=1), jnp.concatenate([h_re, h_im], axis=1)], axis=0
    )
    high = h_all.astype(bf16)
    rest = h_all - high.astype(f32)
    mid = rest.astype(bf16)
    wh[0] = high
    wh[1] = mid
    wh[2] = (rest - mid.astype(f32)).astype(bf16)

    def mask(j, carry):
        row_time = order[r * B + j]
        for kk in range(B):
            keep = jnp.where(order[c * B + kk] >= row_time, jnp.float32(1), jnp.float32(0)).astype(bf16)
            g[j, kk] = g[j, kk] * keep
        return carry

    lax.fori_loop(0, B, mask, 0)

    def hamiltonian(left):
        acc = jnp.dot(left, wh[2], preferred_element_type=f32)
        acc += jnp.dot(left, wh[1], preferred_element_type=f32)
        acc += jnp.dot(left, wh[0], preferred_element_type=f32)
        return acc

    def flow(finish, f, phase, after):
        turns = []
        spreads = []
        for ch in range(NC):
            finish(ch)
            turns.append(turn((piece_a, piece_b)[phase].at[near(ch)], f, phase, ch))
            if ch > 0:
                turns[ch - 1].wait_recv()
                spreads.append(spread(f, phase, ch - 1))
        turns[NC - 1].wait_recv()
        spreads.append(spread(f, phase, NC - 1))
        for ch in range(NC):
            after(ch)
        return spreads

    def finish_a(ch):
        total = comb_a[core_piece(ch, z)]
        for copy, d in zip(a_z[ch], FAR):
            copy.wait_recv()
            total = total + z_a[d - 1, near(ch)]
        piece_a[near(ch)] = total

    def after_a(ch):
        base = piece_a[near(ch)]
        shift_b[near(ch)] = hamiltonian(base)

    a_all = flow(finish_a, f_prev, 0, after_a)

    def self_energy(f, ch):
        first, count = CHUNKS[ch]
        for n in range(first, first + count):
            re = f[n * O:(n + 1) * O, :O]
            im = f[n * O:(n + 1) * O, O:]
            both = jnp.concatenate([re, im], axis=0)
            turned = jnp.dot(both, select, preferred_element_type=f32).astype(bf16)
            turned = jnp.concatenate([turned[:O], turned[O:]], axis=1)
            turned = jnp.dot(select, turned, preferred_element_type=f32)
            t_re = turned[:, :O]
            t_im = turned[:, O:]
            factor = strength * (t_re * t_re + t_im * t_im)
            s_re = (factor * re.astype(f32)).astype(bf16)
            s_im = (factor * im.astype(f32)).astype(bf16)
            w[n, :O, :O] = -s_im
            w[n, :O, O:] = s_re
            w[n, O:, :O] = s_re
            w[n, O:, O:] = s_im

    def contract(first, count, ch, fresh):
        at = rows(first * O, count * O)
        start, number = CHUNKS[ch]
        for kk in range(start, start + number):
            left = jnp.concatenate(
                [g[pl.ds(first, count), kk, i].reshape(count * O, O) for i in range(2)], axis=1
            )
            term = jnp.dot(left, w[kk], preferred_element_type=f32)
            if fresh and kk == start:
                part[at] = term
            else:
                part[at] += term

    for ch in range(NC):
        received(a_all[ch])
        self_energy(f_prev, ch)
        if ch < NC - 1:
            contract(0, B, ch, ch == 0)
    b_core = []

    b_z = []
    for ch in range(NC):
        first, n = CHUNKS[ch]
        contract(first + (1 - k) * (n // 2), n // 2, NC - 1, False)
        b_core.append(to_other(part.at[half(ch, 1 - k)], core_b.at[core_near(ch)], 1, ch))
    for ch in range(NC):
        first, n = CHUNKS[ch]
        contract(first + k * (n // 2), n // 2, NC - 1, False)
        b_core[ch].wait_recv()
        comb_b[core_near(ch)] = part[half(ch, k)] + core_b[core_near(ch)]
        code(
            lambda zz: comb_b[first * 64 + zz * n * 8:first * 64 + (zz + 1) * n * 8],
            near(ch), code_b, scale, 0, ch,
        )
        b_z.append(over_z(code_b, near(ch), z_b, 0, ch))
    for copy in b_core:
        copy.wait_send()
    sent[:] = [copy for copy in sent if not any(copy is done for done in b_core)]

    def finish_b(ch):
        first, n = CHUNKS[ch]
        total = summed(comb_b[core_piece(ch, z)], b_z[ch], near(ch), z_b, 0, ch)
        base = piece_a[near(ch)].astype(f32)
        piece_b[near(ch)] = (base + time_step * (shift_b[near(ch)] + total)).astype(bf16)

    def after_b(ch):
        base = piece_a[near(ch)].astype(f32)
        rest = (2 / time_step) * base + shift_b[near(ch)] + hamiltonian(piece_b[near(ch)])
        part[piece(ch, q_out)] += rest

    b_all = flow(finish_b, f_new, 1, after_b)

    for ch in range(NC):
        received(b_all[ch])
        self_energy(f_new, ch)
        if ch < NC - 1:
            contract(0, B, ch, False)
    d_core = []

    d_z = []

    def over_z_d(ch):
        first, n = CHUNKS[ch]
        d_core[ch].wait_recv()
        comb_d[ch][...] = send_d[ch][k] + core_d[ch][...]
        at = pl.ds(first * 16, n * 16)
        code(lambda zz: comb_d[ch][zz], at, code_d, scale, 1, ch)
        d_z.append(over_z(code_d, at, z_d, 1, ch))

    for ch in range(NC):
        first, n = CHUNKS[ch]
        if ch > 0:
            over_z_d(ch - 1)
        contract(first, n, NC - 1, False)
        for j in range(first, first + n):
            for o in range(2):
                turned = part[j * O:(j + 1) * O, o * O:(o + 1) * O].T.reshape(8, 2, 8, O)
                at = pl.ds((2 * (j - first) + o) * 8, 8)
                for kk in range(2):
                    send_d[ch][kk, :, at] = turned[:, kk]
        d_core.append(to_other(send_d[ch].at[1 - k], core_d[ch], 2, ch))
    over_z_d(NC - 1)
    for ch in range(NC):
        first, n = CHUNKS[ch]
        total = summed(comb_d[ch][z], d_z[ch], pl.ds(first * 16, n * 16), z_d, 1, ch)
        out[first:first + n] = (0.5 * time_step) * total.reshape(n, 2, 8, O)

    for copy in sent:
        copy.wait_send()


def shards(g_hist, hamiltonian, interaction, partner, order):
    bf16 = jnp.bfloat16
    f32 = jnp.float32
    vmem = pltpu.VMEM
    dma = pltpu.SemaphoreType.DMA
    return pl.pallas_call(
        kernel,
        out_shape=jax.ShapeDtypeStruct((B, 2, 8, O), f32),
        in_specs=[pl.BlockSpec(memory_space=pltpu.HBM)] * 5,
        out_specs=pl.BlockSpec(memory_space=pltpu.VMEM),
        scratch_shapes=[
            vmem((B, B, 2, O, O), bf16),
            vmem((2, O, O), f32),
            vmem((1, O), f32),
            vmem((1, O), jnp.int32),
            pltpu.SMEM((16 * B,), jnp.int32),
            vmem((ROWS, 2 * O), bf16),
            vmem((ROWS // 2, 2 * O), bf16),
            vmem((ROWS // 2, 2 * O), bf16),
            vmem((7, ROWS // 16, 2 * O), bf16),
            vmem((ROWS // 16, 2 * O), bf16),
            vmem((ROWS, 2 * O), bf16),
            vmem((B, 2 * O, 2 * O), bf16),
            vmem((3, 2 * O, 2 * O), bf16),
            vmem((ROWS, 2 * O), f32),
            vmem((ROWS // 2, 2 * O), f32),
            vmem((ROWS // 2, 2 * O), f32),
            vmem((8, ROWS // 16, 2 * O), jnp.int16),
            vmem((7, ROWS // 16, 2 * O), jnp.int16),
            vmem((2, NC, 8, 8, O), f32),
            vmem((2, NC, 7, 8, O), f32),
            vmem((ROWS // 16, 2 * O), f32),
            vmem((ROWS // 16, 2 * O), bf16),
            vmem((ROWS, 2 * O), bf16),
            vmem((8, 16 * B, O), jnp.int16),
            vmem((7, 16 * B, O), jnp.int16),
            dma((B,)),
            dma((4,)),
            dma((3, NC)),
            dma((3, NC)),
            dma((NC, 7)),
            dma((NC, 7)),
            dma((2, NC, 7)),
            dma((2, NC, 7)),
            dma((2, NC, 7)),
            dma((2, NC, 7)),
            dma((2, NC)),
            dma((2, NC)),
            dma((2, NC, 15)),
            dma((2, NC, 15)),
        ]
        + [vmem((2, 8, 16 * n, O), f32) for _, n in CHUNKS]
        + [vmem((8, 16 * n, O), f32) for _, n in CHUNKS] * 2,
        compiler_params=pltpu.CompilerParams(
            collective_id=0, has_side_effects=True, vmem_limit_bytes=60 * 2**20
        ),
    )(g_hist, hamiltonian, interaction.reshape(1, O), partner.reshape(1, O), order)


def solution(mesh):
    in_specs = (P("row", "col", None, None, None), P(), P(), P(), P())
    out_specs = P("row", None, "col", None)
    return jax.shard_map(shards, mesh=mesh, in_specs=in_specs, out_specs=out_specs, check_vma=False)
```
